1024 devices in a mesh: branch: 64 (over y, x), leaf: 16 (over z, core).
Axes of the slice: x: 8, y: 8, z: 8, core: 2. Of those that a mesh axis runs over, the one named last changes fastest.
Arguments:
- vectors: bfloat16 [16, 1048576], P(None, ('branch', 'leaf')), may hold values from -6 to 6
- near_ids: int32 [16384, 8], P(('branch', 'leaf')), may hold values from 0 to 16383, as said below
- coup_ids: int32 [16384, 8], P(('branch', 'leaf')), may hold values from 0 to 16383, as said below
- near_blocks: bfloat16 [16384, 8, 4096], P(('branch', 'leaf')), may hold values from -0.25 to 0.25
- coup_blocks: bfloat16 [16384, 8, 4096], P(('branch', 'leaf')), may hold values from -0.25 to 0.25
- col_basis: bfloat16 [16384, 4096], P(('branch', 'leaf')), may hold values from -0.75 to 0.75
- row_basis: bfloat16 [16384, 4096], P(('branch', 'leaf')), may hold values from -0.5 to 0.5
- col_transfer: bfloat16 [16384, 4096], P(('branch', 'leaf')), may hold values from -0.046875 to 0.046875
- row_transfer: bfloat16 [16384, 4096], P(('branch', 'leaf')), may hold values from -0.75 to 0.75
- top_coupling: float32 [64, 64, 4096], P('branch'), may hold values from -0.09375 to 0.09375
Outputs:
- product: float32 [16, 1048576], P(None, ('branch', 'leaf'))
The draws below stay inside these ranges and needn't reach their ends.
Inputs may be any that keep to these rules, and one draw needn't show every extreme that they name: Leaf g lies on device g // 16 (branch index major, leaf index minor). Entry 0 of row i of near_ids is i; every other entry of near_ids names a leaf whose device has the same leaf index as row i's device and a branch index equal to it or one away cyclically. Over near_ids and coup_ids together, the rows of one device name at most 4 distinct leaves of any one other device; some device names exactly 4 of one peer in every draw. `coup_ids`: every entry names a leaf whose device has the same leaf index as row i's device and a branch index two or more away cyclically; the bound of 4 distinct leaves a device pair stated for near_ids covers both lists together.
All inputs are finite; a program needn't handle non-finite values.
Results may differ from the reference program's by a relative error of at most 0.0034.
Values may be sent and summed in bfloat16 or wider, within the bound.
No kernel may reach another device: no remote copies, remote signals or barrier semaphores. Data moves between devices by JAX's collectives and lax.ppermute only.
A program may use at most 32 MiB of HBM per device.

```python
import jax
import jax.numpy as jnp
from jax import lax

LEAF = 64
RANK = 64
RHS = 16
NEAR = 8
COUP = 8
CAP = 4
LEAF_DEV = 16
SUBTREE = 256
LEAVES = 16384
NPTS = 1048576
N_BRANCH = 64
N_LEAF = 16


def window_starts(key):
    return jax.random.randint(key, (N_BRANCH * N_LEAF, N_BRANCH), 0, LEAF_DEV, dtype=jnp.int32)


def leaf_frame():
    leaf_ids = jnp.arange(LEAF_DEV * N_LEAF * N_BRANCH, dtype=jnp.int32)
    device = leaf_ids // LEAF_DEV
    return (leaf_ids, device, device // N_LEAF, device % N_LEAF)


def choose_leaf(starts, device, branch, column, peer_branch, window_step, local_pick):
    window_start = starts[device, peer_branch]
    far_pick = (window_start + window_step) % LEAF_DEV
    chosen = jnp.where(peer_branch == branch, local_pick, far_pick)
    return ((peer_branch * N_LEAF + column) * LEAF_DEV + chosen).astype(jnp.int32)


def draw_near_ids(key, part):
    starts = window_starts(key)
    key = jax.random.fold_in(key, 11)
    key_hop, key_step, key_local = jax.random.split(key, 3)
    leaf_ids, device, branch, column = leaf_frame()
    leaves = leaf_ids.shape[0]
    hop_size = jax.random.randint(key_hop, (leaves, NEAR - 1), -1, 2, dtype=jnp.int32)
    window_step = jax.random.randint(key_step, (leaves, NEAR - 1), 0, CAP, dtype=jnp.int32)
    local_pick = jax.random.randint(key_local, (leaves, NEAR - 1), 0, LEAF_DEV, dtype=jnp.int32)
    peer_branch = (branch[:, None] + hop_size + N_BRANCH) % N_BRANCH
    slot_index = jnp.arange(NEAR - 1, dtype=jnp.int32)[None, :]
    forced = (leaf_ids % LEAF_DEV == 0)[:, None] & (slot_index < CAP)
    peer_branch = jnp.where(forced, (branch[:, None] + 1) % N_BRANCH, peer_branch)
    window_step = jnp.where(forced, slot_index, window_step)
    chosen = choose_leaf(starts, device[:, None], branch[:, None], column[:, None], peer_branch, window_step, local_pick)
    return jnp.concatenate([leaf_ids[:, None], chosen], axis=1)


def draw_coup_ids(key, part):
    starts = window_starts(key)
    key = jax.random.fold_in(key, 12)
    key_hop, key_step = jax.random.split(key, 2)
    leaf_ids, device, branch, column = leaf_frame()
    leaves = leaf_ids.shape[0]
    hop_size = jax.random.randint(key_hop, (leaves, COUP), 2, N_BRANCH - 1, dtype=jnp.int32)
    window_step = jax.random.randint(key_step, (leaves, COUP), 0, CAP, dtype=jnp.int32)
    peer_branch = (branch[:, None] + hop_size) % N_BRANCH
    return choose_leaf(starts, device[:, None], branch[:, None], column[:, None], peer_branch, window_step, window_step)


def level_of(rng, extent, cuts, low, high):
    level, own = 1.0, jax.random.fold_in(rng, 6)
    for position, blocks in cuts:
        steps = jnp.exp(jax.random.uniform(jax.random.fold_in(own, position), (blocks,), jnp.float32, low / len(cuts), high / len(cuts)))
        level = level * jnp.repeat(steps, extent[position] // blocks).reshape([-1 if axis == position else 1 for axis in range(len(extent))])
    return level


def gaussian(own_key, extent, width, reach, cuts=(), held_as=jnp.bfloat16):
    values = jax.random.normal(own_key, extent, jnp.float32) * width
    if len(cuts) > 0:
        values = level_of(own_key, extent, cuts, -0.22, 0.18) * values
    return jnp.clip(values, min=-reach, max=reach).astype(held_as)


def setup_inputs(seed: int = 0) -> dict:
    seeds = jax.random.split(jax.random.key(seed), 11)
    vectors = gaussian(seeds[0], (RHS, NPTS), 1.0, 6.0, ((1, 1024),))
    near_ids = draw_near_ids(jax.random.fold_in(seeds[10], 71), 0)
    coup_ids = draw_coup_ids(jax.random.fold_in(seeds[10], 71), 0)
    near_blocks = gaussian(seeds[3], (LEAVES, NEAR, LEAF * LEAF), (NEAR * LEAF) ** -0.5, 0.25, ((0, 1024),))
    coup_blocks = gaussian(seeds[4], (LEAVES, COUP, RANK * RANK), (COUP * RANK) ** -0.5, 0.25, ((0, 1024),))
    col_basis = gaussian(seeds[5], (LEAVES, LEAF * RANK), LEAF ** -0.5, 0.75, ((0, 1024),))
    row_basis = gaussian(seeds[6], (LEAVES, LEAF * RANK), (2 * RANK) ** -0.5, 0.5, ((0, 1024),))
    col_transfer = gaussian(seeds[7], (LEAVES, RANK * RANK), (RANK * LEAF_DEV * N_LEAF) ** -0.5, 0.046875, ((0, 1024),))
    row_transfer = gaussian(seeds[8], (LEAVES, RANK * RANK), RANK ** -0.5, 0.75, ((0, 1024),))
    top_coupling = gaussian(seeds[9], (N_BRANCH, N_BRANCH, RANK * RANK), (N_BRANCH * RANK) ** -0.5, 0.09375, ((0, 64),), jnp.float32)
    return dict(vectors=vectors, near_ids=near_ids, coup_ids=coup_ids, near_blocks=near_blocks, coup_blocks=coup_blocks, col_basis=col_basis, row_basis=row_basis, col_transfer=col_transfer, row_transfer=row_transfer, top_coupling=top_coupling)


def reference(vectors, near_ids, coup_ids, near_blocks, coup_blocks, col_basis, row_basis, col_transfer, row_transfer, top_coupling):
    leaves = near_ids.shape[0]
    leaf_vectors = vectors.reshape(RHS, leaves, LEAF).transpose(1, 0, 2)
    basis_in = col_basis.reshape(leaves, LEAF, RANK).astype(jnp.float32)
    coeffs = jnp.einsum("lpk,lrp->lrk", basis_in, leaf_vectors.astype(jnp.float32)).astype(jnp.bfloat16)
    transfer_up = col_transfer.reshape(leaves, RANK, RANK).astype(jnp.float32)
    lifted = jnp.einsum("lkc,lrk->lrc", transfer_up, coeffs.astype(jnp.float32))
    roots = lifted.reshape(N_BRANCH, SUBTREE, RHS, RANK).sum(axis=1)
    top_blocks = top_coupling.reshape(N_BRANCH, N_BRANCH, RANK, RANK)
    top_coeffs = jnp.einsum("bdac,drc->bra", top_blocks, roots, precision=lax.Precision.HIGHEST).astype(jnp.bfloat16)

    def one_subtree(index):
        offset = index * SUBTREE
        near_here = lax.dynamic_slice_in_dim(near_ids, offset, SUBTREE, 0)
        coup_here = lax.dynamic_slice_in_dim(coup_ids, offset, SUBTREE, 0)
        blocks_near = lax.dynamic_slice_in_dim(near_blocks, offset, SUBTREE, 0).reshape(SUBTREE, NEAR, LEAF, LEAF)
        blocks_coup = lax.dynamic_slice_in_dim(coup_blocks, offset, SUBTREE, 0).reshape(SUBTREE, COUP, RANK, RANK)
        basis_out = lax.dynamic_slice_in_dim(row_basis, offset, SUBTREE, 0).reshape(SUBTREE, LEAF, RANK)
        transfer_down = lax.dynamic_slice_in_dim(row_transfer, offset, SUBTREE, 0).reshape(SUBTREE, RANK, RANK)
        near_vectors = leaf_vectors[near_here]
        near_terms = jnp.einsum("inpq,inrq->irp", blocks_near.astype(jnp.float32), near_vectors.astype(jnp.float32))
        far_coeffs = coeffs[coup_here]
        inner_terms = jnp.einsum("inab,inrb->ira", blocks_coup.astype(jnp.float32), far_coeffs.astype(jnp.float32))
        top_here = lax.dynamic_index_in_dim(top_coeffs, index, 0, keepdims=False)
        inner_terms = inner_terms + jnp.einsum("iac,rc->ira", transfer_down.astype(jnp.float32), top_here.astype(jnp.float32))
        inner_terms = inner_terms.astype(jnp.bfloat16)
        return near_terms + jnp.einsum("ipa,ira->irp", basis_out.astype(jnp.float32), inner_terms.astype(jnp.float32))

    blocks_out = lax.map(one_subtree, jnp.arange(N_BRANCH, dtype=jnp.int32))
    return blocks_out.reshape(leaves, RHS, LEAF).transpose(1, 0, 2).reshape(RHS, leaves * LEAF)
```

```python
import jax
import jax.numpy as jnp
from jax import lax
from jax.experimental import pallas as pl
from jax.experimental.pallas import tpu as pltpu
from jax.sharding import PartitionSpec as P

LEAF = 64
RANK = 64
RHS = 16
NEAR = 8
COUP = 8
CAP = 4
LEAF_DEV = 16
N_BRANCH = 64
N_LEAF = 16
SLOTS = N_BRANCH * CAP
PAIRS = LEAF // 2
MIB = 1024 * 1024

f32 = jnp.float32
bf16 = jnp.bfloat16
i32 = jnp.int32


def dot(a, b, contract=((1,), (0,))):
    return lax.dot_general(a, b, (contract, ((), ())), preferred_element_type=f32)


def dot_t(a, b):
    return dot(a, b, ((1,), (1,)))


def iota(shape, axis):
    return lax.broadcasted_iota(i32, shape, axis)


def hot(condition):
    return condition.astype(f32).astype(bf16)


def split_rows(source, scratch, count, which):
    return scratch[pl.ds(which, PAIRS, stride=count), :].astype(bf16)


def up_kernel(
    near_ref, coup_ref, vectors_ref, basis_ref, transfer_ref, table_ref, named_ref, out_ref, held_b, held_t
):
    for t in range(PAIRS):
        rows = slice(t * LEAF_DEV, (t + 1) * LEAF_DEV)
        lanes = slice(t * 128, (t + 1) * 128)
        held_b[rows, :] = basis_ref[:, lanes].astype(f32)
        held_t[rows, :] = transfer_ref[:, lanes].astype(f32)
    parity = [hot(iota((LEAF, PAIRS), 0) == 2 * iota((LEAF, PAIRS), 1) + h) for h in range(2)]
    x = jnp.concatenate(
        [vectors_ref[:, l * LEAF : (l + 1) * LEAF] for l in range(LEAF_DEV)], axis=0
    )
    x_parts = [dot(x, m).astype(bf16) for m in parity]
    coeffs = []
    for l in range(LEAF_DEV):
        rows = slice(l * RHS, (l + 1) * RHS)
        both = jnp.concatenate([part[rows] for part in x_parts], axis=0)
        got = dot(both, split_rows(basis_ref, held_b, LEAF_DEV, l))
        c = got[:RHS, :RANK] + got[RHS:, RANK:]
        c = c.astype(bf16)
        coeffs.append(c)
        c = c.astype(f32)
        v = x[rows].astype(f32)
        table_ref[l] = jnp.concatenate([c, c], axis=1)
        table_ref[LEAF_DEV + l] = jnp.concatenate([v, v], axis=1)
    c_all = jnp.concatenate(coeffs, axis=0)
    c_parts = [dot(c_all, m).astype(bf16) for m in parity]
    total = jnp.zeros((2 * RHS, 128), f32)
    for l in range(LEAF_DEV):
        rows = slice(l * RHS, (l + 1) * RHS)
        both = jnp.concatenate([part[rows] for part in c_parts], axis=0)
        total = total + dot(both, split_rows(transfer_ref, held_t, LEAF_DEV, l))
    root = total[:RHS, :RANK] + total[RHS:, RANK:]
    flat = jnp.concatenate([root[: RHS // 2], root[RHS // 2 :]], axis=1)
    high = flat.astype(bf16).astype(f32)
    parts = jnp.concatenate([high, flat - high], axis=0)
    named = jnp.zeros((N_BRANCH, 128), f32)
    for ids_ref in (near_ref, coup_ref):
        for entry in range(NEAR):
            ids = ids_ref[entry : entry + 1, :]
            owner_hot = hot((ids >> 8) == iota((N_BRANCH, LEAF_DEV), 0))
            within_hot = hot((ids & (LEAF_DEV - 1)) == iota((128, LEAF_DEV), 0))
            named = named + dot_t(owner_hot, within_hot)
    named = jnp.minimum(named, 1.0)
    named_ref[...] = named
    for peer in range(N_BRANCH):
        mask = jnp.broadcast_to(named[peer : peer + 1], (8, 128))
        out_ref[peer] = jnp.concatenate([parts, mask], axis=0).astype(bf16)


def prepare_kernel(
    me_ref, near_ref, coup_ref, named_ref, blocks_n, blocks_c, down_ref, basis_ref,
    near_out, coup_out, down_out, basis_out, place_ref, held, held_r,
):
    named = named_ref[...].astype(bf16)
    before = hot(iota((128, 128), 0) < iota((128, 128), 1))
    rank_of = dot(named, before).astype(bf16)
    for which, ids_ref in enumerate((near_ref, coup_ref)):
        for entry in range(NEAR):
            ids = ids_ref[entry : entry + 1, :]
            owner, within = ids >> 8, ids & (LEAF_DEV - 1)
            owner_hot = hot(owner == iota((N_BRANCH, LEAF_DEV), 0))
            rank = dot(rank_of, owner_hot, ((0,), (0,)))
            rank = jnp.where(within == iota((128, LEAF_DEV), 0), rank, 0.0)
            rank = jnp.sum(rank, axis=0, keepdims=True).astype(i32)
            row = which * NEAR + entry
            place_ref[row : row + 1, :] = jnp.where(owner == me_ref[0], SLOTS + within, owner * CAP + rank)
    for source, target in ((down_ref, down_out), (basis_ref, basis_out)):
        for t in range(PAIRS):
            held_r[t * LEAF_DEV : (t + 1) * LEAF_DEV, :] = source[:, t * 128 : (t + 1) * 128].astype(f32)
        for i in range(LEAF_DEV):
            target[i * PAIRS : (i + 1) * PAIRS, :] = split_rows(source, held_r, LEAF_DEV, i)

    def one_leaf(i, carry):
        for side, (source, target) in enumerate(((blocks_n, near_out), (blocks_c, coup_out))):
            for t in range(PAIRS):
                held[side, t * NEAR : (t + 1) * NEAR, :] = source[i, :, t * 128 : (t + 1) * 128].astype(f32)
            for j in range(NEAR):
                target[i, :, j * 128 : (j + 1) * 128] = held[side, pl.ds(j, PAIRS, stride=NEAR), :].astype(bf16)
        return carry

    lax.fori_loop(0, LEAF_DEV, one_leaf, 0)


def pick_kernel(me_ref, incoming_ref, table_ref, prepared_ref, out_ref, shares_ref, index_v, index_s, sem):
    wanted = jnp.max(incoming_ref[...].astype(f32)[:, 16:24, :], axis=1)
    turn = hot(iota((N_BRANCH, 128), 0) == iota((N_BRANCH, 128), 1))
    wanted = dot(wanted.astype(bf16), turn, ((0,), (0,)))
    before = hot(iota((128, 128), 1) < iota((128, 128), 0))
    order = wanted * (dot(before, wanted.astype(bf16)) + 1.0)
    hop = (iota((1, 128), 1) - me_ref[0] + N_BRANCH) % N_BRANCH
    base = jnp.where((hop == 1) | (hop == N_BRANCH - 1), LEAF_DEV, 0)
    leaf = iota((128, 128), 0)
    picks = [
        jnp.sum(jnp.where(order == k + 1.0, leaf, 0), axis=0, keepdims=True) + base for k in range(CAP)
    ]
    index_v[...] = jnp.concatenate(picks + picks, axis=0)
    copy = pltpu.make_async_copy(index_v, index_s, sem)
    copy.start()
    copy.wait()
    left = iota((RHS, 128), 1) < LEAF

    def one_peer(p, carry):
        tiles = [
            jnp.where(left, table_ref[index_s[k, p]], table_ref[index_s[k + 1, p]]) for k in range(0, CAP, 2)
        ]
        out_ref[p] = jnp.concatenate(tiles, axis=0).astype(bf16)
        return carry

    lax.fori_loop(0, N_BRANCH, one_peer, 0, unroll=8)
    for p in range(N_BRANCH):
        parts = incoming_ref[p].astype(f32)
        flat = parts[:8] + parts[8:16]
        shares_ref[p] = jnp.concatenate([flat[:, :RANK], flat[:, RANK:]], axis=0)


def share_kernel(folded_ref, received_ref, out_ref):
    folded = folded_ref[...]
    flat = jnp.concatenate([folded[: RHS // 2], folded[RHS // 2 :]], axis=1)
    out_ref[...] = jnp.broadcast_to(flat[None], out_ref.shape)


def leaves_kernel(place_ref, received_ref, table_ref, near_blocks, coup_blocks, near_out, coup_out, wide):
    lane = iota((RHS, 128), 1)
    half = lane // LEAF
    for i in range(LEAF_DEV):
        for side, (blocks, target) in enumerate(((near_blocks, near_out), (coup_blocks, coup_out))):
            for j in range(NEAR):
                place = place_ref[side * NEAR + j, i]
                tile = received_ref[jnp.minimum(place, SLOTS - 1) // 2].astype(f32)
                tile = jnp.where(half == place % 2, tile, pltpu.roll(tile, LEAF, 1))
                if side == 0:
                    own = table_ref[LEAF_DEV + jnp.maximum(place - SLOTS, 0)]
                    tile = jnp.where(place >= SLOTS, own, tile)
                pair = jnp.concatenate(
                    [jnp.where(half == 0, tile, 0.0), jnp.where(half == 1, tile, 0.0)], axis=0
                )
                wide[i % 2, side, :, j * 128 : (j + 1) * 128] = pair.astype(bf16)
            target[:, i * PAIRS : (i + 1) * PAIRS] = dot_t(wide[i % 2, side], blocks[i])


def down_kernel(shares_ref, near_ref, coup_ref, down_ref, basis_ref, out_ref):
    columns = LEAF_DEV * PAIRS
    top = jnp.sum(shares_ref[...], axis=0)
    top = jnp.concatenate([top[:, :RANK], top[:, RANK:]], axis=0).astype(bf16).astype(f32)
    zero = jnp.zeros((RHS, RANK), f32)
    wide = jnp.concatenate(
        [jnp.concatenate([top, zero], axis=1), jnp.concatenate([zero, top], axis=1)], axis=0
    ).astype(bf16)
    inner = (coup_ref[...] + dot_t(wide, down_ref[...])).astype(bf16)
    block = columns // 2
    order = [
        hot(
            (iota((block, 2 * block), 0) // PAIRS == iota((block, 2 * block), 1) // LEAF)
            & (2 * (iota((block, 2 * block), 0) % PAIRS) + h == iota((block, 2 * block), 1) % LEAF)
        )
        for h in range(2)
    ]

    def in_order(halves):
        return sum(dot(part, m) for part, m in zip(halves, order))

    stacked = [
        jnp.concatenate([inner[h * RHS : (h + 1) * RHS, :block], inner[h * RHS : (h + 1) * RHS, block:]], axis=0)
        for h in range(2)
    ]
    natural = in_order(stacked)
    left = iota((RHS, 128), 1) < LEAF
    pieces = []
    for i in range(LEAF_DEV):
        rows = slice((i // 8) * RHS, (i // 8 + 1) * RHS)
        pair = natural[rows, ((i % 8) // 2) * 128 : ((i % 8) // 2 + 1) * 128]
        other = pltpu.roll(pair, LEAF, 1)
        mine, swapped = (pair, other) if i % 2 == 0 else (other, pair)
        both = jnp.concatenate([jnp.where(left, mine, 0.0), jnp.where(left, 0.0, swapped)], axis=0).astype(bf16)
        pieces.append(dot_t(both, basis_ref[i * PAIRS : (i + 1) * PAIRS, :]))
    result = near_ref[...] + jnp.concatenate(pieces, axis=1)
    high = result.astype(bf16).astype(f32)
    middle = (result - high).astype(bf16).astype(f32)
    parts = [part.astype(bf16) for part in (high, middle, result - high - middle)]
    halves = [
        jnp.concatenate(
            [part[h * RHS : (h + 1) * RHS, b * block : (b + 1) * block] for part in parts for b in range(2)],
            axis=0,
        )
        for h in range(2)
    ]
    ordered = in_order(halves)
    for b in range(2):
        rows = [ordered[(2 * k + b) * RHS : (2 * k + b + 1) * RHS] for k in range(3)]
        out_ref[:, b * 2 * block : (b + 1) * 2 * block] = rows[0] + rows[1] + rows[2]


def body(
    vectors,
    near_ids,
    coup_ids,
    near_blocks,
    coup_blocks,
    col_basis,
    row_basis,
    col_transfer,
    row_transfer,
    top_coupling,
):
    vmem = pl.BlockSpec(memory_space=pltpu.VMEM)
    smem = pl.BlockSpec(memory_space=pltpu.SMEM)
    anywhere = pl.BlockSpec(memory_space=pl.ANY)
    struct = jax.ShapeDtypeStruct

    def params(mib):
        return pltpu.CompilerParams(vmem_limit_bytes=mib * MIB)

    me = lax.axis_index("branch").astype(i32).reshape(1)
    near_t, coup_t = near_ids.T, coup_ids.T

    table, named, outgoing = pl.pallas_call(
        up_kernel,
        out_shape=(
            struct((2 * LEAF_DEV, RHS, 128), f32),
            struct((N_BRANCH, 128), f32),
            struct((N_BRANCH, 24, 128), bf16),
        ),
        in_specs=[vmem] * 5,
        out_specs=(vmem,) * 3,
        scratch_shapes=[pltpu.VMEM((PAIRS * LEAF_DEV, 128), f32)] * 2,
        compiler_params=params(32),
        name="up",
    )(near_t, coup_t, vectors, col_basis, col_transfer)

    incoming = lax.all_to_all(outgoing, "branch", 0, 0, tiled=True)

    wide = NEAR * 128
    near_wide, coup_wide, down_wide, basis_wide, place = pl.pallas_call(
        prepare_kernel,
        out_shape=(
            struct((LEAF_DEV, PAIRS, wide), bf16),
            struct((LEAF_DEV, PAIRS, wide), bf16),
            struct((LEAF_DEV * PAIRS, 128), bf16),
            struct((LEAF_DEV * PAIRS, 128), bf16),
            struct((NEAR + COUP, LEAF_DEV), i32),
        ),
        in_specs=[smem] + [vmem] * 7,
        out_specs=(vmem,) * 5,
        scratch_shapes=[
            pltpu.VMEM((2, PAIRS * NEAR, 128), f32),
            pltpu.VMEM((PAIRS * LEAF_DEV, 128), f32),
        ],
        compiler_params=params(16),
        name="prepare",
    )(me, near_t, coup_t, named, near_blocks, coup_blocks, row_transfer, row_basis)

    sent, shares = pl.pallas_call(
        pick_kernel,
        out_shape=(struct((N_BRANCH, CAP // 2 * RHS, 128), bf16), struct((N_BRANCH, RHS, RANK), f32)),
        in_specs=[smem, vmem, vmem, anywhere],
        out_specs=(vmem, vmem),
        scratch_shapes=[
            pltpu.VMEM((8, 128), i32),
            pltpu.SMEM((8, 128), i32),
            pltpu.SemaphoreType.DMA,
        ],
        compiler_params=params(8),
        name="pick",
    )(me, incoming, table, place)
    received = lax.all_to_all(sent, "branch", 0, 0, tiled=True)

    top_rows = top_coupling.reshape(N_BRANCH, RANK, RANK)
    folded = jnp.einsum("mac,mrc->ra", top_rows, shares, precision=lax.Precision.HIGHEST)
    spread = pl.pallas_call(
        share_kernel,
        out_shape=struct((N_LEAF, 8, 128), f32),
        in_specs=[vmem, anywhere],
        out_specs=vmem,
        compiler_params=params(4),
        name="share",
    )(folded, received)
    gathered = lax.all_to_all(spread, "leaf", 0, 0, tiled=True)

    columns = LEAF_DEV * PAIRS
    near_sum, coup_sum = pl.pallas_call(
        leaves_kernel,
        out_shape=(struct((2 * RHS, columns), f32),) * 2,
        in_specs=[smem] + [vmem] * 4,
        out_specs=(vmem, vmem),
        scratch_shapes=[pltpu.VMEM((2, 2, 2 * RHS, wide), bf16)],
        compiler_params=params(12),
        cost_estimate=pl.CostEstimate(flops=70_000_000, bytes_accessed=4_000_000, transcendentals=0),
        name="leaves",
    )(place, received.reshape(SLOTS // 2, RHS, 128), table, near_wide, coup_wide)

    return pl.pallas_call(
        down_kernel,
        out_shape=struct((RHS, LEAF_DEV * LEAF), f32),
        in_specs=[vmem] * 5,
        out_specs=vmem,
        compiler_params=params(12),
        name="down",
    )(gathered, near_sum, coup_sum, down_wide, basis_wide)


def solution(mesh):
    in_specs = (
        P(None, ("branch", "leaf")),
        P(("branch", "leaf"), None),
        P(("branch", "leaf"), None),
        P(("branch", "leaf"), None, None),
        P(("branch", "leaf"), None, None),
        P(("branch", "leaf"), None),
        P(("branch", "leaf"), None),
        P(("branch", "leaf"), None),
        P(("branch", "leaf"), None),
        P("branch", None, None),
    )
    out_specs = P(None, ("branch", "leaf"))
    return jax.shard_map(body, mesh=mesh, in_specs=in_specs, out_specs=out_specs, check_vma=False)
```

```python
import jax
import jax.numpy as jnp
from jax import lax
from jax.experimental import pallas as pl
from jax.experimental.pallas import tpu as pltpu
from jax.sharding import PartitionSpec as P

LEAF = 64
RANK = 64
RHS = 16
NEAR = 8
COUP = 8
CAP = 4
LEAF_DEV = 16
N_BRANCH = 64
N_LEAF = 16
SLOTS = N_BRANCH * CAP
PAIRS = LEAF // 2
MIB = 1024 * 1024

f32 = jnp.float32
bf16 = jnp.bfloat16
i32 = jnp.int32


def dot(a, b, contract=((1,), (0,))):
    return lax.dot_general(a, b, (contract, ((), ())), preferred_element_type=f32)


def dot_t(a, b):
    return dot(a, b, ((1,), (1,)))


def iota(shape, axis):
    return lax.broadcasted_iota(i32, shape, axis)


def hot(condition):
    return condition.astype(f32).astype(bf16)


def split_rows(source, scratch, count, which):
    return scratch[pl.ds(which, PAIRS, stride=count), :].astype(bf16)


def up_kernel(
    near_ref, coup_ref, vectors_ref, basis_ref, transfer_ref, table_ref, named_ref, out_ref, held_b, held_t
):
    for t in range(PAIRS):
        rows = slice(t * LEAF_DEV, (t + 1) * LEAF_DEV)
        lanes = slice(t * 128, (t + 1) * 128)
        held_b[rows, :] = basis_ref[:, lanes].astype(f32)
        held_t[rows, :] = transfer_ref[:, lanes].astype(f32)
    parity = [hot(iota((LEAF, PAIRS), 0) == 2 * iota((LEAF, PAIRS), 1) + h) for h in range(2)]
    x = jnp.concatenate(
        [vectors_ref[:, l * LEAF : (l + 1) * LEAF] for l in range(LEAF_DEV)], axis=0
    )
    x_parts = [dot(x, m).astype(bf16) for m in parity]
    coeffs = []
    for l in range(LEAF_DEV):
        rows = slice(l * RHS, (l + 1) * RHS)
        both = jnp.concatenate([part[rows] for part in x_parts], axis=0)
        got = dot(both, split_rows(basis_ref, held_b, LEAF_DEV, l))
        c = got[:RHS, :RANK] + got[RHS:, RANK:]
        c = c.astype(bf16)
        coeffs.append(c)
        c = c.astype(f32)
        v = x[rows].astype(f32)
        table_ref[l] = jnp.concatenate([c, c], axis=1)
        table_ref[LEAF_DEV + l] = jnp.concatenate([v, v], axis=1)
    c_all = jnp.concatenate(coeffs, axis=0)
    c_parts = [dot(c_all, m).astype(bf16) for m in parity]
    total = jnp.zeros((2 * RHS, 128), f32)
    for l in range(LEAF_DEV):
        rows = slice(l * RHS, (l + 1) * RHS)
        both = jnp.concatenate([part[rows] for part in c_parts], axis=0)
        total = total + dot(both, split_rows(transfer_ref, held_t, LEAF_DEV, l))
    root = total[:RHS, :RANK] + total[RHS:, RANK:]
    flat = jnp.concatenate([root[: RHS // 2], root[RHS // 2 :]], axis=1)
    high = flat.astype(bf16).astype(f32)
    parts = jnp.concatenate([high, flat - high], axis=0)
    named = jnp.zeros((N_BRANCH, 128), f32)
    for ids_ref in (near_ref, coup_ref):
        for entry in range(NEAR):
            ids = ids_ref[entry : entry + 1, :]
            owner_hot = hot((ids >> 8) == iota((N_BRANCH, LEAF_DEV), 0))
            within_hot = hot((ids & (LEAF_DEV - 1)) == iota((128, LEAF_DEV), 0))
            named = named + dot_t(owner_hot, within_hot)
    named = jnp.minimum(named, 1.0)
    named_ref[...] = named
    for peer in range(N_BRANCH):
        mask = jnp.broadcast_to(named[peer : peer + 1], (8, 128))
        out_ref[peer] = jnp.concatenate([parts, mask], axis=0).astype(bf16)


def prepare_kernel(
    me_ref, near_ref, coup_ref, named_ref, blocks_n, blocks_c, down_ref, basis_ref,
    near_out, coup_out, down_out, basis_out, place_ref, held, held_r,
):
    named = named_ref[...].astype(bf16)
    before = hot(iota((128, 128), 0) < iota((128, 128), 1))
    rank_of = dot(named, before).astype(bf16)
    for which, ids_ref in enumerate((near_ref, coup_ref)):
        for entry in range(NEAR):
            ids = ids_ref[entry : entry + 1, :]
            owner, within = ids >> 8, ids & (LEAF_DEV - 1)
            owner_hot = hot(owner == iota((N_BRANCH, LEAF_DEV), 0))
            rank = dot(rank_of, owner_hot, ((0,), (0,)))
            rank = jnp.where(within == iota((128, LEAF_DEV), 0), rank, 0.0)
            rank = jnp.sum(rank, axis=0, keepdims=True).astype(i32)
            row = which * NEAR + entry
            place_ref[row : row + 1, :] = jnp.where(owner == me_ref[0], SLOTS + within, owner * CAP + rank)
    for source, target in ((down_ref, down_out), (basis_ref, basis_out)):
        for t in range(PAIRS):
            held_r[t * LEAF_DEV : (t + 1) * LEAF_DEV, :] = source[:, t * 128 : (t + 1) * 128].astype(f32)
        for i in range(LEAF_DEV):
            target[i * PAIRS : (i + 1) * PAIRS, :] = split_rows(source, held_r, LEAF_DEV, i)

    def one_leaf(i, carry):
        for side, (source, target) in enumerate(((blocks_n, near_out), (blocks_c, coup_out))):
            for t in range(PAIRS):
                held[side, t * NEAR : (t + 1) * NEAR, :] = source[i, :, t * 128 : (t + 1) * 128].astype(f32)
            for j in range(NEAR):
                target[i, :, j * 128 : (j + 1) * 128] = held[side, pl.ds(j, PAIRS, stride=NEAR), :].astype(bf16)
        return carry

    lax.fori_loop(0, LEAF_DEV, one_leaf, 0)


def pick_kernel(
    me_ref, incoming_ref, table_ref, prepared_ref, top_ref, out_ref, shares_ref, index_v, index_s, sem
):
    wanted = jnp.max(incoming_ref[...].astype(f32)[:, 16:24, :], axis=1)
    turn = hot(iota((N_BRANCH, 128), 0) == iota((N_BRANCH, 128), 1))
    wanted = dot(wanted.astype(bf16), turn, ((0,), (0,)))
    before = hot(iota((128, 128), 1) < iota((128, 128), 0))
    order = wanted * (dot(before, wanted.astype(bf16)) + 1.0)
    hop = (iota((1, 128), 1) - me_ref[0] + N_BRANCH) % N_BRANCH
    base = jnp.where((hop == 1) | (hop == N_BRANCH - 1), LEAF_DEV, 0)
    leaf = iota((128, 128), 0)
    picks = [
        jnp.sum(jnp.where(order == k + 1.0, leaf, 0), axis=0, keepdims=True) + base for k in range(CAP)
    ]
    index_v[...] = jnp.concatenate(picks + picks, axis=0)
    copy = pltpu.make_async_copy(index_v, index_s, sem)
    copy.start()
    copy.wait()
    left = iota((RHS, 128), 1) < LEAF

    def one_peer(p, carry):
        tiles = [
            jnp.where(left, table_ref[index_s[k, p]], table_ref[index_s[k + 1, p]]) for k in range(0, CAP, 2)
        ]
        out_ref[p] = jnp.concatenate(tiles, axis=0).astype(bf16)
        return carry

    lax.fori_loop(0, N_BRANCH, one_peer, 0, unroll=8)
    for p in range(N_BRANCH):
        parts = incoming_ref[p].astype(f32)
        flat = parts[:8] + parts[8:16]
        shares_ref[p] = jnp.concatenate([flat[:, :RANK], flat[:, RANK:]], axis=0)


def finish_kernel(
    place_ref, shares_ref, received_ref, near_blocks, coup_blocks, table_hbm, down_hbm, basis_hbm, out_ref,
    own_ref, down_ref, basis_ref, wide, near_ref, coup_ref, sems,
):
    def fetch(n, source, target):
        copy = pltpu.make_async_copy(source, target, sems.at[n])
        copy.start()
        return copy

    first = fetch(0, table_hbm.at[pl.ds(LEAF_DEV, LEAF_DEV)], own_ref)
    last = [fetch(1, down_hbm, down_ref), fetch(2, basis_hbm, basis_ref)]
    first.wait()

    half = iota((RHS, 128), 1) // LEAF
    for i in range(LEAF_DEV):
        for side, (blocks, target) in enumerate(((near_blocks, near_ref), (coup_blocks, coup_ref))):
            for j in range(NEAR):
                place = place_ref[side * NEAR + j, i]
                tile = received_ref[jnp.minimum(place, SLOTS - 1) // 2].astype(f32)
                tile = jnp.where(half == place % 2, tile, pltpu.roll(tile, LEAF, 1))
                if side == 0:
                    own = own_ref[jnp.maximum(place - SLOTS, 0)]
                    tile = jnp.where(place >= SLOTS, own, tile)
                pair = jnp.concatenate(
                    [jnp.where(half == 0, tile, 0.0), jnp.where(half == 1, tile, 0.0)], axis=0
                )
                wide[i % 2, side, :, j * 128 : (j + 1) * 128] = pair.astype(bf16)
            target[:, i * PAIRS : (i + 1) * PAIRS] = dot_t(wide[i % 2, side], blocks[i])
    for copy in last:
        copy.wait()

    columns = LEAF_DEV * PAIRS
    top = jnp.sum(shares_ref[...], axis=0)
    top = jnp.concatenate([top[:, :RANK], top[:, RANK:]], axis=0).astype(bf16).astype(f32)
    zero = jnp.zeros((RHS, RANK), f32)
    wide = jnp.concatenate(
        [jnp.concatenate([top, zero], axis=1), jnp.concatenate([zero, top], axis=1)], axis=0
    ).astype(bf16)
    inner = (coup_ref[...] + dot_t(wide, down_ref[...])).astype(bf16)
    block = columns // 2
    order = [
        hot(
            (iota((block, 2 * block), 0) // PAIRS == iota((block, 2 * block), 1) // LEAF)
            & (2 * (iota((block, 2 * block), 0) % PAIRS) + h == iota((block, 2 * block), 1) % LEAF)
        )
        for h in range(2)
    ]

    def in_order(halves):
        return sum(dot(part, m) for part, m in zip(halves, order))

    stacked = [
        jnp.concatenate([inner[h * RHS : (h + 1) * RHS, :block], inner[h * RHS : (h + 1) * RHS, block:]], axis=0)
        for h in range(2)
    ]
    natural = in_order(stacked)
    left = iota((RHS, 128), 1) < LEAF
    pieces = []
    for i in range(LEAF_DEV):
        rows = slice((i // 8) * RHS, (i // 8 + 1) * RHS)
        pair = natural[rows, ((i % 8) // 2) * 128 : ((i % 8) // 2 + 1) * 128]
        other = pltpu.roll(pair, LEAF, 1)
        mine, swapped = (pair, other) if i % 2 == 0 else (other, pair)
        both = jnp.concatenate([jnp.where(left, mine, 0.0), jnp.where(left, 0.0, swapped)], axis=0).astype(bf16)
        pieces.append(dot_t(both, basis_ref[i * PAIRS : (i + 1) * PAIRS, :]))
    result = near_ref[...] + jnp.concatenate(pieces, axis=1)
    high = result.astype(bf16).astype(f32)
    middle = (result - high).astype(bf16).astype(f32)
    parts = [part.astype(bf16) for part in (high, middle, result - high - middle)]
    halves = [
        jnp.concatenate(
            [part[h * RHS : (h + 1) * RHS, b * block : (b + 1) * block] for part in parts for b in range(2)],
            axis=0,
        )
        for h in range(2)
    ]
    ordered = in_order(halves)
    for b in range(2):
        rows = [ordered[(2 * k + b) * RHS : (2 * k + b + 1) * RHS] for k in range(3)]
        out_ref[:, b * 2 * block : (b + 1) * 2 * block] = rows[0] + rows[1] + rows[2]


def body(
    vectors,
    near_ids,
    coup_ids,
    near_blocks,
    coup_blocks,
    col_basis,
    row_basis,
    col_transfer,
    row_transfer,
    top_coupling,
):
    vmem = pl.BlockSpec(memory_space=pltpu.VMEM)
    smem = pl.BlockSpec(memory_space=pltpu.SMEM)
    anywhere = pl.BlockSpec(memory_space=pl.ANY)
    struct = jax.ShapeDtypeStruct

    def params(mib):
        return pltpu.CompilerParams(vmem_limit_bytes=int(mib * MIB))

    me = lax.axis_index("branch").astype(i32).reshape(1)
    near_t, coup_t = near_ids.T, coup_ids.T

    table, named, outgoing = pl.pallas_call(
        up_kernel,
        out_shape=(
            struct((2 * LEAF_DEV, RHS, 128), f32),
            struct((N_BRANCH, 128), f32),
            struct((N_BRANCH, 24, 128), bf16),
        ),
        in_specs=[vmem] * 5,
        out_specs=(vmem,) * 3,
        scratch_shapes=[pltpu.VMEM((PAIRS * LEAF_DEV, 128), f32)] * 2,
        compiler_params=params(56),
        name="up",
    )(near_t, coup_t, vectors, col_basis, col_transfer)

    incoming = lax.all_to_all(outgoing, "branch", 0, 0, tiled=True)

    wide = NEAR * 128
    near_wide, coup_wide, down_wide, basis_wide, place = pl.pallas_call(
        prepare_kernel,
        out_shape=(
            struct((LEAF_DEV, PAIRS, wide), bf16),
            struct((LEAF_DEV, PAIRS, wide), bf16),
            struct((LEAF_DEV * PAIRS, 128), bf16),
            struct((LEAF_DEV * PAIRS, 128), bf16),
            struct((NEAR + COUP, LEAF_DEV), i32),
        ),
        in_specs=[smem] + [vmem] * 7,
        out_specs=(vmem,) * 5,
        scratch_shapes=[
            pltpu.VMEM((2, PAIRS * NEAR, 128), f32),
            pltpu.VMEM((PAIRS * LEAF_DEV, 128), f32),
        ],
        compiler_params=params(53.5),
        name="prepare",
    )(me, near_t, coup_t, named, near_blocks, coup_blocks, row_transfer, row_basis)

    top_rows = top_coupling.reshape(N_BRANCH, RANK, RANK)
    sent, shares = pl.pallas_call(
        pick_kernel,
        out_shape=(struct((N_BRANCH, CAP // 2 * RHS, 128), bf16), struct((N_BRANCH, RHS, RANK), f32)),
        in_specs=[smem, vmem, vmem, anywhere, anywhere],
        out_specs=(vmem, vmem),
        scratch_shapes=[
            pltpu.VMEM((8, 128), i32),
            pltpu.SMEM((8, 128), i32),
            pltpu.SemaphoreType.DMA,
        ],
        compiler_params=params(53.3),
        name="pick",
    )(me, incoming, table, place, top_rows)
    received = lax.all_to_all(sent, "branch", 0, 0, tiled=True)

    folded = jnp.einsum("mac,mrc->ra", top_rows, shares, precision=lax.Precision.HIGHEST)
    flat = jnp.concatenate([folded[: RHS // 2], folded[RHS // 2 :]], axis=1)
    gathered = lax.all_gather(flat[None], "leaf", axis=0, tiled=True)

    columns = LEAF_DEV * PAIRS
    return pl.pallas_call(
        finish_kernel,
        out_shape=struct((RHS, LEAF_DEV * LEAF), f32),
        in_specs=[smem] + [vmem] * 4 + [anywhere] * 3,
        out_specs=vmem,
        scratch_shapes=[
            pltpu.VMEM((LEAF_DEV, RHS, 128), f32),
            pltpu.VMEM((columns, 128), bf16),
            pltpu.VMEM((columns, 128), bf16),
            pltpu.VMEM((2, 2, 2 * RHS, wide), bf16),
            pltpu.VMEM((2 * RHS, columns), f32),
            pltpu.VMEM((2 * RHS, columns), f32),
            pltpu.SemaphoreType.DMA((3,)),
        ],
        compiler_params=params(50),
        name="finish",
    )(
        place, gathered, received.reshape(SLOTS // 2, RHS, 128), near_wide, coup_wide, table, down_wide, basis_wide
    )


def solution(mesh):
    in_specs = (
        P(None, ("branch", "leaf")),
        P(("branch", "leaf"), None),
        P(("branch", "leaf"), None),
        P(("branch", "leaf"), None, None),
        P(("branch", "leaf"), None, None),
        P(("branch", "leaf"), None),
        P(("branch", "leaf"), None),
        P(("branch", "leaf"), None),
        P(("branch", "leaf"), None),
        P("branch", None, None),
    )
    out_specs = P(None, ("branch", "leaf"))
    return jax.shard_map(body, mesh=mesh, in_specs=in_specs, out_specs=out_specs, check_vma=False)
```

```python
import jax
import jax.numpy as jnp
from jax import lax
from jax.experimental import pallas as pl
from jax.experimental.pallas import tpu as pltpu
from jax.sharding import PartitionSpec as P

LEAF = 64
RANK = 64
RHS = 16
NEAR = 8
COUP = 8
CAP = 4
LEAF_DEV = 16
N_BRANCH = 64
N_LEAF = 16
SLOTS = N_BRANCH * CAP
PAIRS = LEAF // 2
MARK = 128 - LEAF_DEV
MIB = 1024 * 1024

f32 = jnp.float32
bf16 = jnp.bfloat16
i32 = jnp.int32


def dot(a, b, contract=((1,), (0,))):
    return lax.dot_general(a, b, (contract, ((), ())), preferred_element_type=f32)


def dot_t(a, b):
    return dot(a, b, ((1,), (1,)))


def iota(shape, axis):
    return lax.broadcasted_iota(i32, shape, axis)


def hot(condition):
    return condition.astype(f32).astype(bf16)


def mask_spot(rows):
    return (iota((rows, 128), 0) == rows - 1) & (iota((rows, 128), 1) >= MARK)


def split_rows(source, scratch, count, which):
    return scratch[pl.ds(which, PAIRS, stride=count), :].astype(bf16)


def up_kernel(
    near_ref, coup_ref, vectors_ref, basis_ref, transfer_ref, table_ref, named_ref, out_ref, held_b, held_t
):
    for t in range(PAIRS):
        rows = slice(t * LEAF_DEV, (t + 1) * LEAF_DEV)
        lanes = slice(t * 128, (t + 1) * 128)
        held_b[rows, :] = basis_ref[:, lanes].astype(f32)
        held_t[rows, :] = transfer_ref[:, lanes].astype(f32)
    parity = [hot(iota((LEAF, PAIRS), 0) == 2 * iota((LEAF, PAIRS), 1) + h) for h in range(2)]
    x = jnp.concatenate(
        [vectors_ref[:, l * LEAF : (l + 1) * LEAF] for l in range(LEAF_DEV)], axis=0
    )
    x_parts = [dot(x, m).astype(bf16) for m in parity]
    coeffs = []
    for l in range(LEAF_DEV):
        rows = slice(l * RHS, (l + 1) * RHS)
        both = jnp.concatenate([part[rows] for part in x_parts], axis=0)
        got = dot(both, split_rows(basis_ref, held_b, LEAF_DEV, l))
        c = got[:RHS, :RANK] + got[RHS:, RANK:]
        c = c.astype(bf16)
        coeffs.append(c)
        c = c.astype(f32)
        v = x[rows].astype(f32)
        table_ref[l] = jnp.concatenate([c, c], axis=1)
        table_ref[LEAF_DEV + l] = jnp.concatenate([v, v], axis=1)
    c_all = jnp.concatenate(coeffs, axis=0)
    c_parts = [dot(c_all, m).astype(bf16) for m in parity]
    total = jnp.zeros((2 * RHS, 128), f32)
    for l in range(LEAF_DEV):
        rows = slice(l * RHS, (l + 1) * RHS)
        both = jnp.concatenate([part[rows] for part in c_parts], axis=0)
        total = total + dot(both, split_rows(transfer_ref, held_t, LEAF_DEV, l))
    root = total[:RHS, :RANK] + total[RHS:, RANK:]
    flat = jnp.concatenate([root[: RHS // 2], root[RHS // 2 :]], axis=1)
    high = flat.astype(bf16).astype(f32)
    parts = jnp.concatenate([high, flat - high], axis=0)
    named = jnp.zeros((N_BRANCH, 128), f32)
    for ids_ref in (near_ref, coup_ref):
        for entry in range(NEAR):
            ids = ids_ref[entry : entry + 1, :]
            owner_hot = hot((ids >> 8) == iota((N_BRANCH, LEAF_DEV), 0))
            within_hot = hot((ids & (LEAF_DEV - 1)) + MARK == iota((128, LEAF_DEV), 0))
            named = named + dot_t(owner_hot, within_hot)
    named = jnp.minimum(named, 1.0)
    named_ref[...] = named
    spot = mask_spot(RHS)
    for peer in range(N_BRANCH):
        mask = jnp.broadcast_to(named[peer : peer + 1], (RHS, 128))
        out_ref[peer] = jnp.where(spot, mask, parts).astype(bf16)


def prepare_kernel(
    me_ref, near_ref, coup_ref, named_ref, blocks_n, blocks_c, down_ref, basis_ref,
    near_out, coup_out, down_out, basis_out, place_ref, held, held_r,
):
    named = named_ref[...].astype(bf16)
    before = hot(iota((128, 128), 0) < iota((128, 128), 1))
    rank_of = dot(named, before).astype(bf16)
    for which, ids_ref in enumerate((near_ref, coup_ref)):
        for entry in range(NEAR):
            ids = ids_ref[entry : entry + 1, :]
            owner, within = ids >> 8, ids & (LEAF_DEV - 1)
            owner_hot = hot(owner == iota((N_BRANCH, LEAF_DEV), 0))
            rank = dot(rank_of, owner_hot, ((0,), (0,)))
            rank = jnp.where(within + MARK == iota((128, LEAF_DEV), 0), rank, 0.0)
            rank = jnp.sum(rank, axis=0, keepdims=True).astype(i32)
            row = which * NEAR + entry
            place_ref[row : row + 1, :] = jnp.where(owner == me_ref[0], SLOTS + within, owner * CAP + rank)
    for source, target in ((down_ref, down_out), (basis_ref, basis_out)):
        for t in range(PAIRS):
            held_r[t * LEAF_DEV : (t + 1) * LEAF_DEV, :] = source[:, t * 128 : (t + 1) * 128].astype(f32)
        for i in range(LEAF_DEV):
            target[i * PAIRS : (i + 1) * PAIRS, :] = split_rows(source, held_r, LEAF_DEV, i)

    def one_leaf(i, carry):
        for side, (source, target) in enumerate(((blocks_n, near_out), (blocks_c, coup_out))):
            for t in range(PAIRS):
                held[side, t * NEAR : (t + 1) * NEAR, :] = source[i, :, t * 128 : (t + 1) * 128].astype(f32)
            for j in range(NEAR):
                target[i, :, j * 128 : (j + 1) * 128] = held[side, pl.ds(j, PAIRS, stride=NEAR), :].astype(bf16)
        return carry

    lax.fori_loop(0, LEAF_DEV, one_leaf, 0)


def pick_kernel(
    me_ref, incoming_ref, table_ref, prepared_ref, top_ref, out_ref, shares_ref, index_v, index_s, sem
):
    spot = mask_spot(8)
    wanted = jnp.sum(jnp.where(spot[None], incoming_ref[...].astype(f32)[:, 8:16, :], 0.0), axis=1)
    turn = hot(iota((N_BRANCH, 128), 0) == iota((N_BRANCH, 128), 1))
    wanted = dot(wanted.astype(bf16), turn, ((0,), (0,)))
    before = hot(iota((128, 128), 1) < iota((128, 128), 0))
    order = wanted * (dot(before, wanted.astype(bf16)) + 1.0)
    hop = (iota((1, 128), 1) - me_ref[0] + N_BRANCH) % N_BRANCH
    base = jnp.where((hop == 1) | (hop == N_BRANCH - 1), LEAF_DEV, 0)
    leaf = iota((128, 128), 0) - MARK
    picks = [
        jnp.sum(jnp.where(order == k + 1.0, leaf, 0), axis=0, keepdims=True) + base for k in range(CAP)
    ]
    index_v[...] = jnp.concatenate(picks + picks, axis=0)
    copy = pltpu.make_async_copy(index_v, index_s, sem)
    copy.start()
    copy.wait()
    left = iota((RHS, 128), 1) < LEAF

    def one_peer(p, carry):
        tiles = [
            jnp.where(left, table_ref[index_s[k, p]], table_ref[index_s[k + 1, p]]) for k in range(0, CAP, 2)
        ]
        out_ref[p] = jnp.concatenate(tiles, axis=0).astype(bf16)
        return carry

    lax.fori_loop(0, N_BRANCH, one_peer, 0, unroll=8)
    for p in range(N_BRANCH):
        parts = incoming_ref[p].astype(f32)
        flat = parts[:8] + jnp.where(spot, 0.0, parts[8:])
        shares_ref[p] = jnp.concatenate([flat[:, :RANK], flat[:, RANK:]], axis=0)


def finish_kernel(
    place_ref, shares_ref, received_ref, near_blocks, coup_hbm, table_hbm, down_hbm, basis_hbm, out_ref,
    own_ref, coup_blocks, down_ref, basis_ref, wide, near_ref, coup_ref, sems,
):
    def fetch(n, source, target):
        copy = pltpu.make_async_copy(source, target, sems.at[n])
        copy.start()
        return copy

    first = fetch(0, table_hbm.at[pl.ds(LEAF_DEV, LEAF_DEV)], own_ref)
    second = fetch(3, coup_hbm, coup_blocks)
    last = [fetch(1, down_hbm, down_ref), fetch(2, basis_hbm, basis_ref)]
    first.wait()

    half = iota((RHS, 128), 1) // LEAF
    for side, (blocks, target) in enumerate(((near_blocks, near_ref), (coup_blocks, coup_ref))):
        if side == 1:
            second.wait()
        for i in range(LEAF_DEV):
            for j in range(NEAR):
                place = place_ref[side * NEAR + j, i]
                tile = received_ref[jnp.minimum(place, SLOTS - 1) // 2].astype(f32)
                tile = jnp.where(half == place % 2, tile, pltpu.roll(tile, LEAF, 1))
                if side == 0:
                    own = own_ref[jnp.maximum(place - SLOTS, 0)]
                    tile = jnp.where(place >= SLOTS, own, tile)
                pair = jnp.concatenate(
                    [jnp.where(half == 0, tile, 0.0), jnp.where(half == 1, tile, 0.0)], axis=0
                )
                wide[i % 2, side, :, j * 128 : (j + 1) * 128] = pair.astype(bf16)
            target[:, i * PAIRS : (i + 1) * PAIRS] = dot_t(wide[i % 2, side], blocks[i])
    for copy in last:
        copy.wait()

    columns = LEAF_DEV * PAIRS
    top = jnp.sum(shares_ref[...], axis=0)
    top = jnp.concatenate([top[:, :RANK], top[:, RANK:]], axis=0).astype(bf16).astype(f32)
    zero = jnp.zeros((RHS, RANK), f32)
    wide = jnp.concatenate(
        [jnp.concatenate([top, zero], axis=1), jnp.concatenate([zero, top], axis=1)], axis=0
    ).astype(bf16)
    inner = (coup_ref[...] + dot_t(wide, down_ref[...])).astype(bf16)
    block = columns // 2
    order = [
        hot(
            (iota((block, 2 * block), 0) // PAIRS == iota((block, 2 * block), 1) // LEAF)
            & (2 * (iota((block, 2 * block), 0) % PAIRS) + h == iota((block, 2 * block), 1) % LEAF)
        )
        for h in range(2)
    ]

    def in_order(halves):
        return sum(dot(part, m) for part, m in zip(halves, order))

    stacked = [
        jnp.concatenate([inner[h * RHS : (h + 1) * RHS, :block], inner[h * RHS : (h + 1) * RHS, block:]], axis=0)
        for h in range(2)
    ]
    natural = in_order(stacked)
    left = iota((RHS, 128), 1) < LEAF
    pieces = []
    for i in range(LEAF_DEV):
        rows = slice((i // 8) * RHS, (i // 8 + 1) * RHS)
        pair = natural[rows, ((i % 8) // 2) * 128 : ((i % 8) // 2 + 1) * 128]
        other = pltpu.roll(pair, LEAF, 1)
        mine, swapped = (pair, other) if i % 2 == 0 else (other, pair)
        both = jnp.concatenate([jnp.where(left, mine, 0.0), jnp.where(left, 0.0, swapped)], axis=0).astype(bf16)
        pieces.append(dot_t(both, basis_ref[i * PAIRS : (i + 1) * PAIRS, :]))
    result = near_ref[...] + jnp.concatenate(pieces, axis=1)
    high = result.astype(bf16).astype(f32)
    middle = (result - high).astype(bf16).astype(f32)
    parts = [part.astype(bf16) for part in (high, middle, result - high - middle)]
    halves = [
        jnp.concatenate(
            [part[h * RHS : (h + 1) * RHS, b * block : (b + 1) * block] for part in parts for b in range(2)],
            axis=0,
        )
        for h in range(2)
    ]
    ordered = in_order(halves)
    for b in range(2):
        rows = [ordered[(2 * k + b) * RHS : (2 * k + b + 1) * RHS] for k in range(3)]
        out_ref[:, b * 2 * block : (b + 1) * 2 * block] = rows[0] + rows[1] + rows[2]


def body(
    vectors,
    near_ids,
    coup_ids,
    near_blocks,
    coup_blocks,
    col_basis,
    row_basis,
    col_transfer,
    row_transfer,
    top_coupling,
):
    vmem = pl.BlockSpec(memory_space=pltpu.VMEM)
    smem = pl.BlockSpec(memory_space=pltpu.SMEM)
    anywhere = pl.BlockSpec(memory_space=pl.ANY)
    struct = jax.ShapeDtypeStruct

    def params(mib):
        return pltpu.CompilerParams(vmem_limit_bytes=int(mib * MIB))

    me = lax.axis_index("branch").astype(i32).reshape(1)
    near_t, coup_t = near_ids.T, coup_ids.T

    table, named, outgoing = pl.pallas_call(
        up_kernel,
        out_shape=(
            struct((2 * LEAF_DEV, RHS, 128), f32),
            struct((N_BRANCH, 128), f32),
            struct((N_BRANCH, RHS, 128), bf16),
        ),
        in_specs=[vmem] * 5,
        out_specs=(vmem,) * 3,
        scratch_shapes=[pltpu.VMEM((PAIRS * LEAF_DEV, 128), f32)] * 2,
        compiler_params=params(56),
        name="up",
    )(near_t, coup_t, vectors, col_basis, col_transfer)

    incoming = lax.all_to_all(outgoing, "branch", 0, 0, tiled=True)

    wide = NEAR * 128
    near_wide, coup_wide, down_wide, basis_wide, place = pl.pallas_call(
        prepare_kernel,
        out_shape=(
            struct((LEAF_DEV, PAIRS, wide), bf16),
            struct((LEAF_DEV, PAIRS, wide), bf16),
            struct((LEAF_DEV * PAIRS, 128), bf16),
            struct((LEAF_DEV * PAIRS, 128), bf16),
            struct((NEAR + COUP, LEAF_DEV), i32),
        ),
        in_specs=[smem] + [vmem] * 7,
        out_specs=(vmem,) * 5,
        scratch_shapes=[
            pltpu.VMEM((2, PAIRS * NEAR, 128), f32),
            pltpu.VMEM((PAIRS * LEAF_DEV, 128), f32),
        ],
        compiler_params=params(53.5),
        name="prepare",
    )(me, near_t, coup_t, named, near_blocks, coup_blocks, row_transfer, row_basis)

    top_rows = top_coupling.reshape(N_BRANCH, RANK, RANK)
    sent, shares = pl.pallas_call(
        pick_kernel,
        out_shape=(struct((N_BRANCH, CAP // 2 * RHS, 128), bf16), struct((N_BRANCH, RHS, RANK), f32)),
        in_specs=[smem, vmem, vmem, anywhere, anywhere],
        out_specs=(vmem, vmem),
        scratch_shapes=[
            pltpu.VMEM((8, 128), i32),
            pltpu.SMEM((8, 128), i32),
            pltpu.SemaphoreType.DMA,
        ],
        compiler_params=params(53.3),
        name="pick",
    )(me, incoming, table, place, top_rows)
    received = lax.all_to_all(sent, "branch", 0, 0, tiled=True)

    folded = jnp.einsum("mac,mrc->ra", top_rows, shares, precision=lax.Precision.HIGHEST)
    flat = jnp.concatenate([folded[: RHS // 2], folded[RHS // 2 :]], axis=1)
    gathered = lax.all_gather(flat[None], "leaf", axis=0, tiled=True)

    columns = LEAF_DEV * PAIRS
    return pl.pallas_call(
        finish_kernel,
        out_shape=struct((RHS, LEAF_DEV * LEAF), f32),
        in_specs=[smem] + [vmem] * 3 + [anywhere] * 4,
        out_specs=vmem,
        scratch_shapes=[
            pltpu.VMEM((LEAF_DEV, RHS, 128), f32),
            pltpu.VMEM((LEAF_DEV, PAIRS, wide), bf16),
            pltpu.VMEM((columns, 128), bf16),
            pltpu.VMEM((columns, 128), bf16),
            pltpu.VMEM((2, 2, 2 * RHS, wide), bf16),
            pltpu.VMEM((2 * RHS, columns), f32),
            pltpu.VMEM((2 * RHS, columns), f32),
            pltpu.SemaphoreType.DMA((4,)),
        ],
        compiler_params=params(51),
        name="finish",
    )(
        place, gathered, received.reshape(SLOTS // 2, RHS, 128), near_wide, coup_wide, table, down_wide, basis_wide
    )


def solution(mesh):
    in_specs = (
        P(None, ("branch", "leaf")),
        P(("branch", "leaf"), None),
        P(("branch", "leaf"), None),
        P(("branch", "leaf"), None, None),
        P(("branch", "leaf"), None, None),
        P(("branch", "leaf"), None),
        P(("branch", "leaf"), None),
        P(("branch", "leaf"), None),
        P(("branch", "leaf"), None),
        P("branch", None, None),
    )
    out_specs = P(None, ("branch", "leaf"))
    return jax.shard_map(body, mesh=mesh, in_specs=in_specs, out_specs=out_specs, check_vma=False)
```

```python
import jax
import jax.numpy as jnp
from jax import lax
from jax.experimental import pallas as pl
from jax.experimental.pallas import tpu as pltpu
from jax.sharding import PartitionSpec as P

LEAF = 64
RANK = 64
RHS = 16
NEAR = 8
COUP = 8
CAP = 4
LEAF_DEV = 16
N_BRANCH = 64
N_LEAF = 16
SLOTS = N_BRANCH * CAP
PAIRS = LEAF // 2
MARK = 128 - LEAF_DEV
MIB = 1024 * 1024

f32 = jnp.float32
bf16 = jnp.bfloat16
i32 = jnp.int32


def dot(a, b, contract=((1,), (0,))):
    return lax.dot_general(a, b, (contract, ((), ())), preferred_element_type=f32)


def dot_t(a, b):
    return dot(a, b, ((1,), (1,)))


def iota(shape, axis):
    return lax.broadcasted_iota(i32, shape, axis)


def hot(condition):
    return condition.astype(f32).astype(bf16)


def mask_spot(rows):
    return (iota((rows, 128), 0) == rows - 1) & (iota((rows, 128), 1) >= MARK)


def split_rows(source, scratch, count, which):
    return scratch[pl.ds(which, PAIRS, stride=count), :].astype(bf16)


def up_kernel(
    near_ref, coup_ref, vectors_ref, basis_ref, transfer_ref, table_ref, named_ref, out_ref, held_b, held_t
):
    for t in range(PAIRS):
        rows = slice(t * LEAF_DEV, (t + 1) * LEAF_DEV)
        lanes = slice(t * 128, (t + 1) * 128)
        held_b[rows, :] = basis_ref[:, lanes].astype(f32)
        held_t[rows, :] = transfer_ref[:, lanes].astype(f32)
    parity = [hot(iota((LEAF, PAIRS), 0) == 2 * iota((LEAF, PAIRS), 1) + h) for h in range(2)]
    x = jnp.concatenate(
        [vectors_ref[:, l * LEAF : (l + 1) * LEAF] for l in range(LEAF_DEV)], axis=0
    )
    x_parts = [dot(x, m).astype(bf16) for m in parity]
    coeffs = []
    for l in range(LEAF_DEV):
        rows = slice(l * RHS, (l + 1) * RHS)
        both = jnp.concatenate([part[rows] for part in x_parts], axis=0)
        got = dot(both, split_rows(basis_ref, held_b, LEAF_DEV, l))
        c = got[:RHS, :RANK] + got[RHS:, RANK:]
        c = c.astype(bf16)
        coeffs.append(c)
        c = c.astype(f32)
        v = x[rows].astype(f32)
        table_ref[l] = jnp.concatenate([c, c], axis=1)
        table_ref[LEAF_DEV + l] = jnp.concatenate([v, v], axis=1)
    c_all = jnp.concatenate(coeffs, axis=0)
    c_parts = [dot(c_all, m).astype(bf16) for m in parity]
    total = jnp.zeros((2 * RHS, 128), f32)
    for l in range(LEAF_DEV):
        rows = slice(l * RHS, (l + 1) * RHS)
        both = jnp.concatenate([part[rows] for part in c_parts], axis=0)
        total = total + dot(both, split_rows(transfer_ref, held_t, LEAF_DEV, l))
    root = total[:RHS, :RANK] + total[RHS:, RANK:]
    flat = jnp.concatenate([root[: RHS // 2], root[RHS // 2 :]], axis=1)
    high = flat.astype(bf16).astype(f32)
    parts = jnp.concatenate([high, flat - high], axis=0)
    named = jnp.zeros((N_BRANCH, 128), f32)
    for ids_ref in (near_ref, coup_ref):
        for entry in range(NEAR):
            ids = ids_ref[entry : entry + 1, :]
            owner_hot = hot((ids >> 8) == iota((N_BRANCH, LEAF_DEV), 0))
            within_hot = hot((ids & (LEAF_DEV - 1)) + MARK == iota((128, LEAF_DEV), 0))
            named = named + dot_t(owner_hot, within_hot)
    named = jnp.minimum(named, 1.0)
    named_ref[...] = named
    spot = mask_spot(RHS)
    for peer in range(N_BRANCH):
        mask = jnp.broadcast_to(named[peer : peer + 1], (RHS, 128))
        out_ref[peer] = jnp.where(spot, mask, parts).astype(bf16)


def prepare_kernel(
    me_ref, near_ref, coup_ref, named_ref, blocks_n, blocks_c, down_ref, basis_ref,
    near_out, coup_out, down_out, basis_out, place_ref, held, held_r,
):
    named = named_ref[...].astype(bf16)
    before = hot(iota((128, 128), 0) < iota((128, 128), 1))
    rank_of = dot(named, before).astype(bf16)
    for which, ids_ref in enumerate((near_ref, coup_ref)):
        for entry in range(NEAR):
            ids = ids_ref[entry : entry + 1, :]
            owner, within = ids >> 8, ids & (LEAF_DEV - 1)
            owner_hot = hot(owner == iota((N_BRANCH, LEAF_DEV), 0))
            rank = dot(rank_of, owner_hot, ((0,), (0,)))
            rank = jnp.where(within + MARK == iota((128, LEAF_DEV), 0), rank, 0.0)
            rank = jnp.sum(rank, axis=0, keepdims=True).astype(i32)
            row = which * NEAR + entry
            place_ref[row : row + 1, :] = jnp.where(owner == me_ref[0], SLOTS + within, owner * CAP + rank)
    for source, target in ((down_ref, down_out), (basis_ref, basis_out)):
        for t in range(PAIRS):
            held_r[t * LEAF_DEV : (t + 1) * LEAF_DEV, :] = source[:, t * 128 : (t + 1) * 128].astype(f32)
        for i in range(LEAF_DEV):
            target[i * PAIRS : (i + 1) * PAIRS, :] = split_rows(source, held_r, LEAF_DEV, i)

    def one_leaf(i, carry):
        for side, (source, target) in enumerate(((blocks_n, near_out), (blocks_c, coup_out))):
            for t in range(PAIRS):
                held[side, t * NEAR : (t + 1) * NEAR, :] = source[i, :, t * 128 : (t + 1) * 128].astype(f32)
            for j in range(NEAR):
                target[i, :, j * 128 : (j + 1) * 128] = held[side, pl.ds(j, PAIRS, stride=NEAR), :].astype(bf16)
        return carry

    lax.fori_loop(0, LEAF_DEV, one_leaf, 0)


def pick_kernel(
    me_ref, incoming_ref, table_ref, prepared_ref, out_ref, shares_ref, index_v, index_s, sem
):
    spot = mask_spot(8)
    wanted = jnp.sum(jnp.where(spot[None], incoming_ref[...].astype(f32)[:, 8:16, :], 0.0), axis=1)
    turn = hot(iota((N_BRANCH, 128), 0) == iota((N_BRANCH, 128), 1))
    wanted = dot(wanted.astype(bf16), turn, ((0,), (0,)))
    before = hot(iota((128, 128), 1) < iota((128, 128), 0))
    order = wanted * (dot(before, wanted.astype(bf16)) + 1.0)
    hop = (iota((1, 128), 1) - me_ref[0] + N_BRANCH) % N_BRANCH
    base = jnp.where((hop == 1) | (hop == N_BRANCH - 1), LEAF_DEV, 0)
    leaf = iota((128, 128), 0) - MARK
    picks = [
        jnp.sum(jnp.where(order == k + 1.0, leaf, 0), axis=0, keepdims=True) + base for k in range(CAP)
    ]
    index_v[...] = jnp.concatenate(picks + picks, axis=0)
    copy = pltpu.make_async_copy(index_v, index_s, sem)
    copy.start()
    copy.wait()
    left = iota((RHS, 128), 1) < LEAF

    def one_peer(p, carry):
        tiles = [
            jnp.where(left, table_ref[index_s[k, p]], table_ref[index_s[k + 1, p]]) for k in range(0, CAP, 2)
        ]
        out_ref[p] = jnp.concatenate(tiles, axis=0).astype(bf16)
        return carry

    lax.fori_loop(0, N_BRANCH, one_peer, 0, unroll=8)
    for p in range(N_BRANCH):
        parts = incoming_ref[p].astype(f32)
        flat = parts[:8] + jnp.where(spot, 0.0, parts[8:])
        shares_ref[p] = jnp.concatenate([flat[:, :RANK], flat[:, RANK:]], axis=0)


def finish_kernel(
    place_ref, shares_ref, received_ref, near_blocks, coup_hbm, table_hbm, down_hbm, basis_hbm, out_ref,
    own_ref, coup_blocks, down_ref, basis_ref, wide, near_ref, coup_ref, sems,
):
    def fetch(n, source, target):
        copy = pltpu.make_async_copy(source, target, sems.at[n])
        copy.start()
        return copy

    first = fetch(0, table_hbm.at[pl.ds(LEAF_DEV, LEAF_DEV)], own_ref)
    second = fetch(3, coup_hbm, coup_blocks)
    last = [fetch(1, down_hbm, down_ref), fetch(2, basis_hbm, basis_ref)]
    first.wait()

    half = iota((RHS, 128), 1) // LEAF
    for side, (blocks, target) in enumerate(((near_blocks, near_ref), (coup_blocks, coup_ref))):
        if side == 1:
            second.wait()
        for i in range(LEAF_DEV):
            for j in range(NEAR):
                place = place_ref[side * NEAR + j, i]
                tile = received_ref[jnp.minimum(place, SLOTS - 1) // 2].astype(f32)
                tile = jnp.where(half == place % 2, tile, pltpu.roll(tile, LEAF, 1))
                if side == 0:
                    own = own_ref[jnp.maximum(place - SLOTS, 0)]
                    tile = jnp.where(place >= SLOTS, own, tile)
                pair = jnp.concatenate(
                    [jnp.where(half == 0, tile, 0.0), jnp.where(half == 1, tile, 0.0)], axis=0
                )
                wide[i % 2, side, :, j * 128 : (j + 1) * 128] = pair.astype(bf16)
            target[:, i * PAIRS : (i + 1) * PAIRS] = dot_t(wide[i % 2, side], blocks[i])
    for copy in last:
        copy.wait()

    columns = LEAF_DEV * PAIRS
    top = jnp.sum(shares_ref[...], axis=0)
    top = jnp.concatenate([top[:, :RANK], top[:, RANK:]], axis=0).astype(bf16).astype(f32)
    zero = jnp.zeros((RHS, RANK), f32)
    wide = jnp.concatenate(
        [jnp.concatenate([top, zero], axis=1), jnp.concatenate([zero, top], axis=1)], axis=0
    ).astype(bf16)
    inner = (coup_ref[...] + dot_t(wide, down_ref[...])).astype(bf16)
    block = columns // 2
    order = [
        hot(
            (iota((block, 2 * block), 0) // PAIRS == iota((block, 2 * block), 1) // LEAF)
            & (2 * (iota((block, 2 * block), 0) % PAIRS) + h == iota((block, 2 * block), 1) % LEAF)
        )
        for h in range(2)
    ]

    def in_order(halves):
        return sum(dot(part, m) for part, m in zip(halves, order))

    stacked = [
        jnp.concatenate([inner[h * RHS : (h + 1) * RHS, :block], inner[h * RHS : (h + 1) * RHS, block:]], axis=0)
        for h in range(2)
    ]
    natural = in_order(stacked)
    left = iota((RHS, 128), 1) < LEAF
    pieces = []
    for i in range(LEAF_DEV):
        rows = slice((i // 8) * RHS, (i // 8 + 1) * RHS)
        pair = natural[rows, ((i % 8) // 2) * 128 : ((i % 8) // 2 + 1) * 128]
        other = pltpu.roll(pair, LEAF, 1)
        mine, swapped = (pair, other) if i % 2 == 0 else (other, pair)
        both = jnp.concatenate([jnp.where(left, mine, 0.0), jnp.where(left, 0.0, swapped)], axis=0).astype(bf16)
        pieces.append(dot_t(both, basis_ref[i * PAIRS : (i + 1) * PAIRS, :]))
    result = near_ref[...] + jnp.concatenate(pieces, axis=1)
    high = result.astype(bf16).astype(f32)
    middle = (result - high).astype(bf16).astype(f32)
    parts = [part.astype(bf16) for part in (high, middle, result - high - middle)]
    halves = [
        jnp.concatenate(
            [part[h * RHS : (h + 1) * RHS, b * block : (b + 1) * block] for part in parts for b in range(2)],
            axis=0,
        )
        for h in range(2)
    ]
    ordered = in_order(halves)
    for b in range(2):
        rows = [ordered[(2 * k + b) * RHS : (2 * k + b + 1) * RHS] for k in range(3)]
        out_ref[:, b * 2 * block : (b + 1) * 2 * block] = rows[0] + rows[1] + rows[2]


def body(
    vectors,
    near_ids,
    coup_ids,
    near_blocks,
    coup_blocks,
    col_basis,
    row_basis,
    col_transfer,
    row_transfer,
    top_coupling,
):
    vmem = pl.BlockSpec(memory_space=pltpu.VMEM)
    smem = pl.BlockSpec(memory_space=pltpu.SMEM)
    anywhere = pl.BlockSpec(memory_space=pl.ANY)
    struct = jax.ShapeDtypeStruct

    def params(mib):
        return pltpu.CompilerParams(vmem_limit_bytes=int(mib * MIB))

    me = lax.axis_index("branch").astype(i32).reshape(1)
    near_t, coup_t = near_ids.T, coup_ids.T

    table, named, outgoing = pl.pallas_call(
        up_kernel,
        out_shape=(
            struct((2 * LEAF_DEV, RHS, 128), f32),
            struct((N_BRANCH, 128), f32),
            struct((N_BRANCH, RHS, 128), bf16),
        ),
        in_specs=[vmem] * 5,
        out_specs=(vmem,) * 3,
        scratch_shapes=[pltpu.VMEM((PAIRS * LEAF_DEV, 128), f32)] * 2,
        compiler_params=params(56),
        name="up",
    )(near_t, coup_t, vectors, col_basis, col_transfer)

    incoming = lax.all_to_all(outgoing, "branch", 0, 0, tiled=True)

    wide = NEAR * 128
    near_wide, coup_wide, down_wide, basis_wide, place = pl.pallas_call(
        prepare_kernel,
        out_shape=(
            struct((LEAF_DEV, PAIRS, wide), bf16),
            struct((LEAF_DEV, PAIRS, wide), bf16),
            struct((LEAF_DEV * PAIRS, 128), bf16),
            struct((LEAF_DEV * PAIRS, 128), bf16),
            struct((NEAR + COUP, LEAF_DEV), i32),
        ),
        in_specs=[smem] + [vmem] * 7,
        out_specs=(vmem,) * 5,
        scratch_shapes=[
            pltpu.VMEM((2, PAIRS * NEAR, 128), f32),
            pltpu.VMEM((PAIRS * LEAF_DEV, 128), f32),
        ],
        compiler_params=params(53.5),
        name="prepare",
    )(me, near_t, coup_t, named, near_blocks, coup_blocks, row_transfer, row_basis)

    top_rows = top_coupling.reshape(N_BRANCH, RANK, RANK)
    sent, shares = pl.pallas_call(
        pick_kernel,
        out_shape=(struct((N_BRANCH, CAP // 2 * RHS, 128), bf16), struct((N_BRANCH, RHS, RANK), f32)),
        in_specs=[smem, vmem, vmem, anywhere],
        out_specs=(vmem, vmem),
        scratch_shapes=[
            pltpu.VMEM((8, 128), i32),
            pltpu.SMEM((8, 128), i32),
            pltpu.SemaphoreType.DMA,
        ],
        compiler_params=params(53.3),
        name="pick",
    )(me, incoming, table, place)
    received = lax.all_to_all(sent, "branch", 0, 0, tiled=True)

    folded = jnp.einsum("mac,mrc->ra", top_rows, shares, precision=lax.Precision.HIGHEST)
    flat = jnp.concatenate([folded[: RHS // 2], folded[RHS // 2 :]], axis=1)
    gathered = lax.all_gather(flat[None], "leaf", axis=0, tiled=True)

    columns = LEAF_DEV * PAIRS
    return pl.pallas_call(
        finish_kernel,
        out_shape=struct((RHS, LEAF_DEV * LEAF), f32),
        in_specs=[smem] + [vmem] * 3 + [anywhere] * 4,
        out_specs=vmem,
        scratch_shapes=[
            pltpu.VMEM((LEAF_DEV, RHS, 128), f32),
            pltpu.VMEM((LEAF_DEV, PAIRS, wide), bf16),
            pltpu.VMEM((columns, 128), bf16),
            pltpu.VMEM((columns, 128), bf16),
            pltpu.VMEM((2, 2, 2 * RHS, wide), bf16),
            pltpu.VMEM((2 * RHS, columns), f32),
            pltpu.VMEM((2 * RHS, columns), f32),
            pltpu.SemaphoreType.DMA((4,)),
        ],
        compiler_params=params(51),
        name="finish",
    )(
        place, gathered, received.reshape(SLOTS // 2, RHS, 128), near_wide, coup_wide, table, down_wide, basis_wide
    )


def solution(mesh):
    in_specs = (
        P(None, ("branch", "leaf")),
        P(("branch", "leaf"), None),
        P(("branch", "leaf"), None),
        P(("branch", "leaf"), None, None),
        P(("branch", "leaf"), None, None),
        P(("branch", "leaf"), None),
        P(("branch", "leaf"), None),
        P(("branch", "leaf"), None),
        P(("branch", "leaf"), None),
        P("branch", None, None),
    )
    out_specs = P(None, ("branch", "leaf"))
    return jax.shard_map(body, mesh=mesh, in_specs=in_specs, out_specs=out_specs, check_vma=False)
```
